512 devices in a mesh: rep: 16 (over x, y_hi), fsdp: 32 (over z, y_lo, core).
Axes of the slice: x: 4, y: 8 (y_hi: 4, y_lo: 2; y = y_hi * 2 + y_lo), z: 8, core: 2. Of those that a mesh axis runs over, the one named last changes fastest.
Arguments:
- partial_grads: bfloat16 [16, 32, 1, 64, 12288], P('rep', 'fsdp'), may hold values from -3 to 3
- momentum: float32 [16, 1, 64, 12288], P('rep', None, None, 'fsdp'), may hold values from -6 to 6
- keep_index: int32 [1, 1, 192, 32], P(None, None, 'fsdp'), may hold values from 0 to 4095, as said below
Outputs:
- new_momentum: float32 [16, 1, 64, 12288], P('rep', None, None, 'fsdp')
- update: float32 [1, 64, 12288], P(None, None, 'fsdp')
The draws below stay inside these ranges and needn't reach their ends.
Inputs may be any that keep to these rules, and one draw needn't show every extreme that they name: `keep_index`: the 32 numbers of each block are distinct.
All inputs are finite; a program needn't handle non-finite values.
Results may differ from the reference program's by a relative error of at most 0.0003.
Values sent between devices are 32-bit elements; how exact they have to be, the bound alone decides.
No kernel may reach another device: no remote copies, remote signals or barrier semaphores. Data moves between devices by JAX's collectives and lax.ppermute only.
A program may use at most 64 MiB of HBM per device.

```python
import jax
import jax.numpy as jnp
from jax import lax

BLOCK = 64
KEEP = 32
LAYERS = 1
COLS = 12288
RBLK = 1
ROWS = 64
COL_BLOCKS = 192
N_REP = 16
N_FSDP = 32


def draw_keep_index(key, part):
    key = jax.random.fold_in(key, 7)
    block_count = LAYERS * RBLK * COL_BLOCKS
    key_list = jax.random.split(key, block_count)

    def pick_block(block_key):
        return jax.random.permutation(block_key, BLOCK * BLOCK)[:KEEP]
    picks = jax.vmap(pick_block)(key_list)
    inner = jax.random.permutation(jax.random.fold_in(key, 1), BLOCK * BLOCK - 2)[:KEEP - 2] + 1
    ends = jnp.array([0, BLOCK * BLOCK - 1], dtype=picks.dtype)
    first_block = jnp.concatenate([ends, inner.astype(picks.dtype)])
    picks = picks.at[0].set(first_block)
    return picks.reshape(LAYERS, RBLK, COL_BLOCKS, KEEP).astype(jnp.int32)


def shard_levels(rng, extent, cuts, smallest, high):
    level, own = 1.0, jax.random.fold_in(rng, 6)
    for position, blocks in cuts:
        draws = jnp.exp(jax.random.uniform(jax.random.fold_in(own, position), (blocks,), jnp.float32, smallest / len(cuts), high / len(cuts)))
        level = level * jnp.repeat(draws, extent[position] // blocks).reshape([-1 if axis == position else 1 for axis in range(len(extent))])
    return level


def gaussian(own_key, dims, spread, limit, cuts=(), kind=jnp.bfloat16):
    gain = shard_levels(own_key, dims, cuts, -0.22, 0.18) if cuts else 1.0
    result = jax.random.normal(own_key, dims, jnp.float32) * spread * gain
    return jnp.minimum(jnp.maximum(result, -limit), limit).astype(kind)


def setup_inputs(seed: int = 0) -> dict:
    splits = jax.random.split(jax.random.key(seed), 4)
    return {
        "partial_grads": gaussian(splits[0], (N_REP, N_FSDP, LAYERS, ROWS, COLS), 0.2, 3.0, ((0, 16), (1, 32))),
        "momentum": gaussian(splits[1], (N_REP, LAYERS, ROWS, COLS), 1.0, 6.0, ((0, 16), (3, 32)), jnp.float32),
        "keep_index": draw_keep_index(jax.random.fold_in(splits[3], 71), 0),
    }


BETA_DECAY = 0.999
SOFTNESS = 0.02

def dct_matrix(block_size):
    frequency = jnp.arange(block_size, dtype=jnp.float32)[:, None]
    sample = jnp.arange(block_size, dtype=jnp.float32)[None, :]
    weights = jnp.where(frequency == 0, jnp.sqrt(1.0 / block_size), jnp.sqrt(2.0 / block_size))
    return weights * jnp.cos(jnp.pi * (2.0 * sample + 1.0) * frequency / (2.0 * block_size))

def to_blocks(field_in, block_size):
    lead_dims = field_in.shape[:-2]
    row_blocks = field_in.shape[-2] // block_size
    col_blocks = field_in.shape[-1] // block_size
    reshaped = field_in.reshape(lead_dims + (row_blocks, block_size, col_blocks, block_size))
    return jnp.swapaxes(reshaped, -3, -2)

def from_blocks(blocked):
    lead_dims = blocked.shape[:-4]
    row_blocks = blocked.shape[-4]
    col_blocks = blocked.shape[-3]
    block_size = blocked.shape[-1]
    return jnp.swapaxes(blocked, -3, -2).reshape(lead_dims + (row_blocks * block_size, col_blocks * block_size))

def forward_dct(blocked, dct_table):
    return jnp.einsum('kn,...nm,jm->...kj', dct_table, blocked, dct_table, precision=lax.Precision.HIGHEST)

def inverse_dct(coeffs, dct_table):
    return jnp.einsum('kn,...kj,jm->...nm', dct_table, coeffs, dct_table, precision=lax.Precision.HIGHEST)

def extract(gradient, momentum, keep_index, dct_table):
    block_size = dct_table.shape[0]
    updated = BETA_DECAY * momentum + gradient
    coeffs = forward_dct(to_blocks(updated, block_size), dct_table)
    flat_coeffs = coeffs.reshape(coeffs.shape[:-2] + (block_size * block_size,))
    one_hot = (keep_index[..., None] == jnp.arange(block_size * block_size, dtype=jnp.int32)).astype(jnp.float32)
    kept_mask = lax.optimization_barrier(jnp.sum(one_hot, axis=-2))
    wanted = jnp.broadcast_to(keep_index, flat_coeffs.shape[:-1] + (keep_index.shape[-1],))
    kept_values = jnp.take_along_axis(flat_coeffs, wanted, axis=-1)
    rebuilt = inverse_dct((flat_coeffs * kept_mask).reshape(coeffs.shape), dct_table)
    return (updated - from_blocks(rebuilt), kept_values, one_hot)

def finish(averaged, one_hot, dct_table):
    block_size = dct_table.shape[0]
    coeff_grid = jnp.einsum('...k,...kj->...j', averaged, one_hot, precision=lax.Precision.HIGHEST)
    blocked = inverse_dct(coeff_grid.reshape(coeff_grid.shape[:-1] + (block_size, block_size)), dct_table)
    direction = from_blocks(blocked)
    return direction / jnp.sqrt(direction * direction + SOFTNESS * SOFTNESS)

def reference(partial_grads, momentum, keep_index):
    start_sum = jnp.zeros(momentum.shape, jnp.float32)

    def add_member(member, running):
        return running + lax.dynamic_index_in_dim(partial_grads, member, 1, False).astype(jnp.float32)
    gradient = lax.fori_loop(0, N_FSDP, add_member, start_sum)
    dct_table = dct_matrix(BLOCK)
    new_momentum, kept_values, one_hot = extract(gradient, momentum, keep_index, dct_table)
    averaged = lax.optimization_barrier(jnp.sum(kept_values, axis=0)) / N_REP
    return (new_momentum, finish(averaged, one_hot, dct_table))
```

```python
import functools

import jax
import jax.numpy as jnp
import numpy as np
from jax import lax
from jax.experimental import pallas as pl
from jax.experimental.pallas import tpu as pltpu
from jax.sharding import Mesh
from jax.sharding import PartitionSpec as P

BLOCK = 64
BETA_DECAY = 0.999
SOFTNESS = 0.02
WIDE = 384
PAIRS = WIDE // 128
KEPT = 64
SIZES = {"x": 4, "yh": 4, "z": 8, "yl": 2, "c": 2}
REP = ("x", "yh")
FSDP = ("z", "yl", "c")
SLOTS = ((0, 4), (0, 3), (1, 3), (0, 2), (1, 2), (0, 1), (1, 1), (0, 0))
HIGHEST = lax.Precision.HIGHEST


def dct_matrix():
    k = np.arange(BLOCK)[:, None]
    n = np.arange(BLOCK)[None, :]
    scale = np.where(k == 0, np.sqrt(1.0 / BLOCK), np.sqrt(2.0 / BLOCK))
    return (scale * np.cos(np.pi * (2 * n + 1) * k / (2 * BLOCK))).astype(np.float32)


def dot(a, b):
    return jnp.dot(a, b, precision=HIGHEST, preferred_element_type=jnp.float32)


def dot_nt(a, b):
    return lax.dot_general(
        a, b, (((1,), (1,)), ((), ())), precision=HIGHEST, preferred_element_type=jnp.float32
    )


def vmem():
    return pl.BlockSpec(memory_space=pltpu.VMEM)


def f32(*shape):
    return jax.ShapeDtypeStruct(shape, jnp.float32)


def params():
    return pltpu.CompilerParams(vmem_limit_bytes=32 * 1024 * 1024)


def chunks(grads_ref, core):
    z = lax.axis_index("z")
    yl = lax.axis_index("yl")
    for slot, (part, distance) in enumerate(SLOTS):
        target = lax.rem(z + 8 + (1 - 2 * core) * distance, 8)
        part = core if part == 0 else 1 - core
        for side in range(2):
            block = 4 * target + 2 * (yl if side == 0 else 1 - yl) + part
            start = pl.multiple_of(block * WIDE, 128)
            yield slot, side, grads_ref[:, pl.ds(start, WIDE)].astype(jnp.float32)


def split_kernel(grads_ref, give_ref, own_ref):
    core = lax.axis_index("c")
    for slot, side, columns in chunks(grads_ref, 1 - core):
        give_ref[slot, side] = columns
    for slot, side, columns in chunks(grads_ref, core):
        own_ref[slot, side] = columns


def split(grads):
    return pl.pallas_call(
        split_kernel,
        out_shape=(f32(len(SLOTS), 2, BLOCK, WIDE),) * 2,
        in_specs=[vmem()],
        out_specs=(vmem(),) * 2,
        compiler_params=params(),
    )(grads)


def table_kernel(index_ref, dct_ref, rows_ref, cols_ref, rows_t_ref):
    dct = dct_ref[...]
    index = index_ref[...]
    size = index.shape[-1]
    iota = lax.broadcasted_iota(jnp.int32, (BLOCK, size), 0)
    hot_u = (iota == lax.shift_right_logical(index, 6)).astype(jnp.float32)
    hot_v = (iota == jnp.bitwise_and(index, 63)).astype(jnp.float32)
    rows_t_ref[...] = dot(dct.T, hot_u)
    rows_ref[...] = dot(hot_u.T, dct)
    wide = dot(hot_v.T, jnp.concatenate([dct, dct], axis=1))
    row = lax.broadcasted_iota(jnp.int32, (size, 128), 0)
    lane = lax.broadcasted_iota(jnp.int32, (size, 128), 1)
    mine = jnp.bitwise_and(lax.shift_right_logical(row, 5), 1) == lax.shift_right_logical(lane, 6)
    cols_ref[...] = jnp.where(mine, wide, 0.0)


def tables(index):
    size = index.shape[-1]
    return pl.pallas_call(
        table_kernel,
        out_shape=(f32(size, BLOCK), f32(size, 128), f32(BLOCK, size)),
        in_specs=[vmem()] * 2,
        out_specs=(vmem(),) * 3,
        compiler_params=params(),
    )(index, dct_matrix())


def join_kernel(own_ref, got_ref, three_ref, four_ref, two_ref, near_ref, near_x_ref, here_ref):
    for ref, first in ((three_ref, 1), (two_ref, 3)):
        for part in range(2):
            ref[part] = own_ref[first + part] + got_ref[first + part]
    for ref, slot in ((four_ref, 0), (near_ref, 5), (near_x_ref, 6), (here_ref, 7)):
        ref[...] = own_ref[slot] + got_ref[slot]


def join(own, got):
    pair = f32(2, BLOCK, WIDE)
    quad = f32(2, 2, BLOCK, WIDE)
    return pl.pallas_call(
        join_kernel,
        out_shape=(quad, pair, quad, pair, pair, pair),
        in_specs=[vmem()] * 2,
        out_specs=(vmem(),) * 6,
        compiler_params=params(),
    )(own, got)


def add_kernel(parts, *refs):
    *ins, out = refs
    terms = [r[...] if p is None else r[p] for r, p in zip(ins, parts)]
    out[...] = functools.reduce(jnp.add, terms)


def add(*terms):
    return pl.pallas_call(
        functools.partial(add_kernel, [p for _, p in terms]),
        out_shape=f32(2, BLOCK, WIDE),
        in_specs=[vmem()] * len(terms),
        out_specs=vmem(),
        compiler_params=params(),
    )(*[a for a, _ in terms])


def merge_kernel(*refs):
    *ins, mine, other = refs
    for side, out in enumerate((mine, other)):
        out[...] = functools.reduce(jnp.add, [r[side] for r in ins])


def merge(*terms):
    return pl.pallas_call(
        merge_kernel,
        out_shape=(f32(BLOCK, WIDE),) * 2,
        in_specs=[vmem()] * len(terms),
        out_specs=(vmem(),) * 2,
        compiler_params=params(),
    )(*terms)


def forward(field, rows, cols):
    total = jnp.zeros((8, KEPT), jnp.float32)
    row = lax.broadcasted_iota(jnp.int32, (8, 128), 0)
    for p in range(PAIRS):
        span = slice(p * KEPT, (p + 1) * KEPT)
        product = dot(rows[span], field[:, p * 128 : (p + 1) * 128]) * cols[span]
        total = total + dot_nt((row == p).astype(jnp.float32), product)
    return total


def inverse(kept, rows_t, cols, p):
    span = slice(p * KEPT, (p + 1) * KEPT)
    return dot(rows_t[:, span] * kept[p : p + 1, :KEPT], cols[span])


def extract_kernel(*refs):
    *terms, momentum_ref, rows_ref, cols_ref, rows_t_ref, new_ref, kept_ref = refs
    updated = functools.reduce(jnp.add, [r[...] for r in terms]) + BETA_DECAY * momentum_ref[...]
    kept = forward(updated, rows_ref, cols_ref)
    tile = jnp.concatenate([kept, jnp.zeros((8, 128 - KEPT), jnp.float32)], axis=1)
    for r in range(kept_ref.shape[0]):
        kept_ref[r] = tile
    for p in range(PAIRS):
        span = slice(p * 128, (p + 1) * 128)
        new_ref[:, span] = updated[:, span] - inverse(kept, rows_t_ref, cols_ref, p)


def extract(groups, *args):
    return pl.pallas_call(
        extract_kernel,
        out_shape=(f32(BLOCK, WIDE), f32(groups, 8, 128)),
        in_specs=[vmem()] * len(args),
        out_specs=(vmem(),) * 2,
        compiler_params=params(),
    )(*args)


def finish_kernel(all_ref, cols_ref, rows_t_ref, upd_ref):
    averaged = jnp.sum(all_ref[...], axis=0) * (1.0 / all_ref.shape[0])
    for p in range(PAIRS):
        direction = inverse(averaged, rows_t_ref, cols_ref, p)
        upd_ref[:, p * 128 : (p + 1) * 128] = direction * lax.rsqrt(
            direction * direction + SOFTNESS * SOFTNESS
        )


def finish(*args):
    return pl.pallas_call(
        finish_kernel,
        out_shape=f32(BLOCK, WIDE),
        in_specs=[vmem()] * 3,
        out_specs=vmem(),
        compiler_params=params(),
    )(*args)


def permutation(hops, flip_yl, flip_c):
    flat = lambda z, yl, c: (z % 8) * 4 + yl * 2 + c
    return [
        (flat(z, yl, c), flat(z + hops * (1 - 2 * c), yl ^ flip_yl, c ^ flip_c))
        for z in range(8)
        for yl in range(2)
        for c in range(2)
    ]


def send(array, hops=0, yl=0, c=0):
    return lax.ppermute(array, FSDP, permutation(hops, yl, c))


def per_device(partial_grads, momentum, keep_index):
    grads = partial_grads.reshape(BLOCK, -1)
    momentum = momentum.reshape(BLOCK, WIDE)

    give, own = split(grads)
    got = send(give, c=1)
    rows, cols, rows_t = tables(keep_index.reshape(1, -1))
    three, four, two, near, near_x, here = join(own, got)
    three = send(three, hops=1)
    four = send(four, hops=2)
    near = send(near, hops=1)
    near_x = send(near_x, hops=1, c=1)
    far_x = send(add((two, 1), (three, 1)), hops=2, c=1)
    far = send(add((two, 0), (three, 0), (four, None)), hops=2)
    mine, other = merge(here, near, near_x, far, far_x)
    other = send(other, yl=1)

    groups = SIZES["x"] * SIZES["yh"]
    new_momentum, kept = extract(groups, mine, other, momentum, rows, cols, rows_t)
    kept = lax.all_to_all(kept, REP, 0, 0, tiled=True)
    update = finish(kept, cols, rows_t)
    return new_momentum.reshape(1, 1, BLOCK, WIDE), update.reshape(1, BLOCK, WIDE)


def solution(mesh):
    inner = Mesh(mesh.devices.reshape(tuple(SIZES.values())), tuple(SIZES))
    in_specs = (
        P(REP, FSDP, None, None, None),
        P(REP, None, None, FSDP),
        P(None, None, FSDP, None),
    )
    out_specs = (P(REP, None, None, FSDP), P(None, None, FSDP))
    return jax.shard_map(
        per_device, mesh=inner, in_specs=in_specs, out_specs=out_specs, check_vma=False
    )
```

```python
import functools

import jax
import jax.numpy as jnp
import numpy as np
from jax import lax
from jax.experimental import pallas as pl
from jax.experimental.pallas import tpu as pltpu
from jax.sharding import Mesh
from jax.sharding import PartitionSpec as P

BLOCK = 64
BETA_DECAY = 0.999
SOFTNESS = 0.02
WIDE = 384
PAIRS = WIDE // 128
KEPT = 64
SIZES = {"x": 4, "yh": 4, "z": 8, "yl": 2, "c": 2}
REP = ("x", "yh")
FSDP = ("z", "yl", "c")
PLACES = (
    [(3, part, side) for part in range(2) for side in range(2)]
    + [(4, 0, side) for side in range(2)]
    + [(k, part, side) for k in (1, 2) for part in range(2) for side in range(2)]
    + [(0, 0, side) for side in range(2)]
)
HIGHEST = lax.Precision.HIGHEST


def dct_matrix():
    k = np.arange(BLOCK)[:, None]
    n = np.arange(BLOCK)[None, :]
    scale = np.where(k == 0, np.sqrt(1.0 / BLOCK), np.sqrt(2.0 / BLOCK))
    return (scale * np.cos(np.pi * (2 * n + 1) * k / (2 * BLOCK))).astype(np.float32)


def dot(a, b, precision=None):
    return jnp.dot(a, b, precision=precision, preferred_element_type=jnp.float32)


def halves(a):
    high = a.astype(jnp.bfloat16)
    return high, (a - high.astype(jnp.float32)).astype(jnp.bfloat16)


def dot_halves(a, b):
    return dot(a[0], b[0]) + (dot(a[1], b[0]) + dot(a[0], b[1]))


def vmem():
    return pl.BlockSpec(memory_space=pltpu.VMEM)


def f32(*shape):
    return jax.ShapeDtypeStruct(shape, jnp.float32)


def bf16(*shape):
    return jax.ShapeDtypeStruct(shape, jnp.bfloat16)


def params():
    return pltpu.CompilerParams(vmem_limit_bytes=32 * 1024 * 1024)


def pick_kernel(other, grads_ref, out_ref):
    z = lax.axis_index("z")
    yl = lax.axis_index("yl")
    core = lax.axis_index("c")
    core = 1 - core if other else core
    for slot, (distance, part, side) in enumerate(PLACES):
        target = lax.rem(z + 8 + (1 - 2 * core) * distance, 8)
        block = 4 * target + 2 * (1 - yl if side else yl) + (1 - core if part else core)
        start = pl.multiple_of(block * WIDE, 128)
        out_ref[slot] = grads_ref[:, pl.ds(start, WIDE)].astype(jnp.float32)


def pick(grads, other):
    return pl.pallas_call(
        functools.partial(pick_kernel, other),
        out_shape=f32(len(PLACES), BLOCK, WIDE),
        in_specs=[vmem()],
        out_specs=vmem(),
        compiler_params=params(),
    )(grads)


def table_kernel(index_ref, dct_ref, u_ref, u_high_ref, u_low_ref, v_t_ref, v_high_ref, v_low_ref):
    dct = dct_ref[...]
    index = index_ref[...]
    size = index.shape[-1]
    iota = lax.broadcasted_iota(jnp.int32, (BLOCK, size), 0)
    hot_u = (iota == lax.shift_right_logical(index, 6)).astype(jnp.float32)
    hot_v = (iota == jnp.bitwise_and(index, 63)).astype(jnp.float32)
    twice = jnp.concatenate([dct, dct], axis=1)
    lane = lax.broadcasted_iota(jnp.int32, (size, 128), 1)
    kept = lax.broadcasted_iota(jnp.int32, (size, 128), 0)
    mine = jnp.bitwise_and(lax.shift_right_logical(kept, 5), 1) == lax.shift_right_logical(lane, 6)
    u = dot(dct.T, hot_u, HIGHEST)
    v = jnp.where(mine, dot(hot_v.T, twice, HIGHEST), 0.0)
    for p in range(PAIRS):
        span = slice(p * KEPT, (p + 1) * KEPT)
        u_ref[p] = u[:, span]
        u_high_ref[p], u_low_ref[p] = halves(u[:, span])
        v_t_ref[p] = v[span].T
        v_high_ref[p], v_low_ref[p] = halves(v[span])


def tables(index):
    square, wide = (PAIRS, BLOCK, KEPT), (PAIRS, KEPT, 128)
    return pl.pallas_call(
        table_kernel,
        out_shape=(f32(*square), bf16(*square), bf16(*square), f32(PAIRS, 128, KEPT), bf16(*wide), bf16(*wide)),
        in_specs=[vmem()] * 2,
        out_specs=(vmem(),) * 6,
        compiler_params=params(),
    )(index, dct_matrix())


def sums_kernel(plan, *refs):
    ins, outs = refs[: len(refs) - len(plan)], refs[len(refs) - len(plan) :]
    for out, rows in zip(outs, plan):
        for row, terms in enumerate(rows):
            out[row] = functools.reduce(jnp.add, [ins[i][j] for i, j in terms])


def sums(plan, *arrays):
    return pl.pallas_call(
        functools.partial(sums_kernel, plan),
        out_shape=tuple(f32(len(rows), BLOCK, WIDE) for rows in plan),
        in_specs=[vmem()] * len(arrays),
        out_specs=(vmem(),) * len(plan),
        compiler_params=params(),
    )(*arrays)


def extract_kernel(*refs):
    *terms, momentum_ref, u_high_ref, u_low_ref, v_t_ref, updated_ref, own_ref, kept_ref = refs
    updated = functools.reduce(jnp.add, [r[0] for r in terms]) + BETA_DECAY * momentum_ref[...]
    updated_ref[...] = updated
    columns = updated.T
    row = lax.broadcasted_iota(jnp.int32, (8, KEPT), 0)
    tile = jnp.zeros((8, KEPT), jnp.float32)
    for p in range(PAIRS):
        field = halves(columns[p * 128 : (p + 1) * 128])
        product = dot_halves(field, (u_high_ref[p], u_low_ref[p])) * v_t_ref[p]
        tile = jnp.where(row == p, jnp.sum(product, axis=0, keepdims=True), tile)
    tile = jnp.concatenate([tile, jnp.zeros((8, 128 - KEPT), jnp.float32)], axis=1)
    own_ref[...] = tile
    for r in range(kept_ref.shape[0]):
        kept_ref[r] = tile


def extract(groups, *args):
    return pl.pallas_call(
        extract_kernel,
        out_shape=(f32(BLOCK, WIDE), f32(8, 128), f32(groups, 8, 128)),
        in_specs=[vmem()] * len(args),
        out_specs=(vmem(),) * 3,
        compiler_params=params(),
    )(*args)


def finish_kernel(updated_ref, own_ref, all_ref, u_ref, v_high_ref, v_low_ref, new_ref, update_ref):
    averaged = jnp.sum(all_ref[...], axis=0) * (1.0 / all_ref.shape[0])
    own = own_ref[...]
    for p in range(PAIRS):
        span = slice(p * 128, (p + 1) * 128)
        v = (v_high_ref[p], v_low_ref[p])
        inverse = lambda kept: dot_halves(halves(u_ref[p] * kept[p : p + 1, :KEPT]), v)
        direction = inverse(averaged)
        update_ref[:, span] = direction * lax.rsqrt(direction * direction + SOFTNESS * SOFTNESS)
        new_ref[:, span] = updated_ref[:, span] - inverse(own)


def finish(*args):
    return pl.pallas_call(
        finish_kernel,
        out_shape=(f32(BLOCK, WIDE),) * 2,
        in_specs=[vmem()] * len(args),
        out_specs=(vmem(),) * 2,
        compiler_params=params(),
    )(*args)


def permutation(hops, flip_yl, flip_c):
    flat = lambda z, yl, c: (z % 8) * 4 + yl * 2 + c
    return [
        (flat(z, yl, c), flat(z + hops * (1 - 2 * c), yl ^ flip_yl, c ^ flip_c))
        for z in range(8)
        for yl in range(2)
        for c in range(2)
    ]


def send(array, hops=0, yl=0, c=0):
    return lax.ppermute(array, FSDP, permutation(hops, yl, c))


def per_device(partial_grads, momentum, keep_index):
    grads = partial_grads.reshape(BLOCK, -1)
    momentum = momentum.reshape(BLOCK, WIDE)

    got = send(pick(grads, True), c=1)
    own = pick(grads, False)
    u, u_high, u_low, v_t, v_high, v_low = tables(keep_index.reshape(1, -1))
    join = lambda *slots: [[(0, i), (1, i)] for i in slots]
    three, four, near, near_x, two, here = sums(
        [join(0, 1, 2, 3), join(4, 5), join(6, 7), join(8, 9), join(10, 11, 12, 13), join(14, 15)], own, got
    )
    three = send(three, hops=1)
    four = send(four, hops=2)
    near = send(near, hops=1)
    near_x = send(near_x, hops=1, c=1)
    (far_x,) = sums([[[(0, 2 + s), (1, 2 + s)] for s in range(2)]], two, three, four)
    far_x = send(far_x, hops=2, c=1)
    far, far_y = sums([[[(0, s), (1, s), (2, s)]] for s in range(2)], two, three, four)
    far = send(far, hops=2)
    far_y = send(far_y, hops=2, yl=1)
    mine, other = sums([[[(i, s) for i in range(4)]] for s in range(2)], here, near, near_x, far_x)
    other = send(other, yl=1)

    groups = SIZES["x"] * SIZES["yh"]
    updated, kept, to_all = extract(groups, mine, other, far, far_y, momentum, u_high, u_low, v_t)
    from_all = lax.all_to_all(to_all, REP, 0, 0, tiled=True)
    new_momentum, update = finish(updated, kept, from_all, u, v_high, v_low)
    return new_momentum.reshape(1, 1, BLOCK, WIDE), update.reshape(1, BLOCK, WIDE)


def solution(mesh):
    inner = Mesh(mesh.devices.reshape(tuple(SIZES.values())), tuple(SIZES))
    in_specs = (
        P(REP, FSDP, None, None, None),
        P(REP, None, None, FSDP),
        P(None, None, FSDP, None),
    )
    out_specs = (P(REP, None, None, FSDP), P(None, None, FSDP))
    return jax.shard_map(
        per_device, mesh=inner, in_specs=in_specs, out_specs=out_specs, check_vma=False
    )
```

```python
import functools

import jax
import jax.numpy as jnp
import numpy as np
from jax import lax
from jax.experimental import pallas as pl
from jax.experimental.pallas import tpu as pltpu
from jax.sharding import Mesh
from jax.sharding import PartitionSpec as P

BLOCK = 64
BETA_DECAY = 0.999
SOFTNESS = 0.02
WIDE = 384
PAIRS = WIDE // 128
KEPT = 64
SIZES = {"x": 4, "yh": 4, "z": 8, "yl": 2, "c": 2}
REP = ("x", "yh")
FSDP = ("z", "yl", "c")
PLACES = (
    [(3, part, side) for part in range(2) for side in range(2)]
    + [(4, 0, side) for side in range(2)]
    + [(k, part, side) for k in (1, 2) for part in range(2) for side in range(2)]
    + [(0, 0, side) for side in range(2)]
)
HIGHEST = lax.Precision.HIGHEST


def dct_matrix():
    k = np.arange(BLOCK)[:, None]
    n = np.arange(BLOCK)[None, :]
    scale = np.where(k == 0, np.sqrt(1.0 / BLOCK), np.sqrt(2.0 / BLOCK))
    return (scale * np.cos(np.pi * (2 * n + 1) * k / (2 * BLOCK))).astype(np.float32)


def dot(a, b, precision=None):
    return jnp.dot(a, b, precision=precision, preferred_element_type=jnp.float32)


def halves(a):
    high = a.astype(jnp.bfloat16)
    return high, (a - high.astype(jnp.float32)).astype(jnp.bfloat16)


def dot_halves(a, b):
    return dot(a[0], b[0]) + (dot(a[1], b[0]) + dot(a[0], b[1]))


def vmem():
    return pl.BlockSpec(memory_space=pltpu.VMEM)


def f32(*shape):
    return jax.ShapeDtypeStruct(shape, jnp.float32)


def bf16(*shape):
    return jax.ShapeDtypeStruct(shape, jnp.bfloat16)


def params():
    return pltpu.CompilerParams(vmem_limit_bytes=32 * 1024 * 1024)


def pick_kernel(other, grads_ref, out_ref):
    z = lax.axis_index("z")
    yl = lax.axis_index("yl")
    core = lax.axis_index("c")
    core = 1 - core if other else core
    for slot, (distance, part, side) in enumerate(PLACES):
        target = lax.rem(z + 8 + (1 - 2 * core) * distance, 8)
        block = 4 * target + 2 * (1 - yl if side else yl) + (1 - core if part else core)
        start = pl.multiple_of(block * WIDE, 128)
        out_ref[slot] = grads_ref[:, pl.ds(start, WIDE)].astype(jnp.float32)


def pick(grads, other):
    return pl.pallas_call(
        functools.partial(pick_kernel, other),
        out_shape=f32(len(PLACES), BLOCK, WIDE),
        in_specs=[vmem()],
        out_specs=vmem(),
        compiler_params=params(),
    )(grads)


def table_kernel(index_ref, dct_ref, u_ref, u_high_ref, u_low_ref, v_t_ref, v_high_ref, v_low_ref):
    dct = dct_ref[...]
    index = index_ref[...]
    size = index.shape[-1]
    iota = lax.broadcasted_iota(jnp.int32, (BLOCK, size), 0)
    hot_u = (iota == lax.shift_right_logical(index, 6)).astype(jnp.float32)
    hot_v = (iota == jnp.bitwise_and(index, 63)).astype(jnp.float32)
    twice = jnp.concatenate([dct, dct], axis=1)
    lane = lax.broadcasted_iota(jnp.int32, (size, 128), 1)
    kept = lax.broadcasted_iota(jnp.int32, (size, 128), 0)
    mine = jnp.bitwise_and(lax.shift_right_logical(kept, 5), 1) == lax.shift_right_logical(lane, 6)
    u = dot(dct.T, hot_u, HIGHEST)
    v = jnp.where(mine, dot(hot_v.T, twice, HIGHEST), 0.0)
    for p in range(PAIRS):
        span = slice(p * KEPT, (p + 1) * KEPT)
        u_ref[p] = u[:, span]
        u_high_ref[p], u_low_ref[p] = halves(u[:, span])
        v_t_ref[p] = v[span].T
        v_high_ref[p], v_low_ref[p] = halves(v[span])


def tables(index):
    square, wide = (PAIRS, BLOCK, KEPT), (PAIRS, KEPT, 128)
    return pl.pallas_call(
        table_kernel,
        out_shape=(f32(*square), bf16(*square), bf16(*square), f32(PAIRS, 128, KEPT), bf16(*wide), bf16(*wide)),
        in_specs=[vmem()] * 2,
        out_specs=(vmem(),) * 6,
        compiler_params=params(),
    )(index, dct_matrix())


def sums_kernel(plan, *refs):
    ins, outs = refs[: len(refs) - len(plan)], refs[len(refs) - len(plan) :]
    for out, rows in zip(outs, plan):
        for row, terms in enumerate(rows):
            out[row] = functools.reduce(jnp.add, [ins[i][j] for i, j in terms])


def sums(plan, *arrays, weight=0):
    return pl.pallas_call(
        functools.partial(sums_kernel, plan),
        out_shape=tuple(f32(len(rows), BLOCK, WIDE) for rows in plan),
        in_specs=[vmem()] * len(arrays),
        out_specs=(vmem(),) * len(plan),
        compiler_params=params(),
        cost_estimate=pl.CostEstimate(flops=0, bytes_accessed=int(weight * 3.69e6) or 1, transcendentals=0),
    )(*arrays)


def extract_kernel(*refs):
    *terms, momentum_ref, u_high_ref, u_low_ref, v_t_ref, updated_ref, own_ref, kept_ref = refs
    updated = functools.reduce(jnp.add, [r[0] for r in terms]) + BETA_DECAY * momentum_ref[...]
    updated_ref[...] = updated
    columns = updated.T
    row = lax.broadcasted_iota(jnp.int32, (8, KEPT), 0)
    tile = jnp.zeros((8, KEPT), jnp.float32)
    for p in range(PAIRS):
        field = halves(columns[p * 128 : (p + 1) * 128])
        product = dot_halves(field, (u_high_ref[p], u_low_ref[p])) * v_t_ref[p]
        tile = jnp.where(row == p, jnp.sum(product, axis=0, keepdims=True), tile)
    tile = jnp.concatenate([tile, jnp.zeros((8, 128 - KEPT), jnp.float32)], axis=1)
    own_ref[...] = tile
    for r in range(kept_ref.shape[0]):
        kept_ref[r] = tile


def extract(groups, *args):
    return pl.pallas_call(
        extract_kernel,
        out_shape=(f32(BLOCK, WIDE), f32(8, 128), f32(groups, 8, 128)),
        in_specs=[vmem()] * len(args),
        out_specs=(vmem(),) * 3,
        compiler_params=params(),
    )(*args)


def finish_kernel(updated_ref, own_ref, all_ref, u_ref, v_high_ref, v_low_ref, new_ref, update_ref):
    averaged = jnp.sum(all_ref[...], axis=0) * (1.0 / all_ref.shape[0])
    own = own_ref[...]
    for p in range(PAIRS):
        span = slice(p * 128, (p + 1) * 128)
        v = (v_high_ref[p], v_low_ref[p])
        inverse = lambda kept: dot_halves(halves(u_ref[p] * kept[p : p + 1, :KEPT]), v)
        direction = inverse(averaged)
        update_ref[:, span] = direction * lax.rsqrt(direction * direction + SOFTNESS * SOFTNESS)
        new_ref[:, span] = updated_ref[:, span] - inverse(own)


def finish(*args):
    return pl.pallas_call(
        finish_kernel,
        out_shape=(f32(BLOCK, WIDE),) * 2,
        in_specs=[vmem()] * len(args),
        out_specs=(vmem(),) * 2,
        compiler_params=params(),
    )(*args)


def permutation(hops, flip_yl, flip_c):
    flat = lambda z, yl, c: (z % 8) * 4 + yl * 2 + c
    return [
        (flat(z, yl, c), flat(z + hops * (1 - 2 * c), yl ^ flip_yl, c ^ flip_c))
        for z in range(8)
        for yl in range(2)
        for c in range(2)
    ]


def send(array, hops=0, yl=0, c=0):
    return lax.ppermute(array, FSDP, permutation(hops, yl, c))


def per_device(partial_grads, momentum, keep_index):
    grads = partial_grads.reshape(BLOCK, -1)
    momentum = momentum.reshape(BLOCK, WIDE)

    got = send(pick(grads, True), c=1)
    own = pick(grads, False)
    u, u_high, u_low, v_t, v_high, v_low = tables(keep_index.reshape(1, -1))
    join = lambda *slots: [[(0, i), (1, i)] for i in slots]
    three, four, near, near_x, two, here = sums(
        [join(0, 1, 2, 3), join(4, 5), join(6, 7), join(8, 9), join(10, 11, 12, 13), join(14, 15)], own, got
    )
    three = send(three, hops=1)
    four = send(four, hops=2)
    near = send(near, hops=1)
    near_x = send(near_x, hops=1, c=1)
    (far_x,) = sums([[[(0, 2 + s), (1, 2 + s)] for s in range(2)]], two, three)
    far_x = send(far_x, hops=2, c=1)
    far, far_y = sums([[[(0, s), (1, s), (2, s)]] for s in range(2)], two, three, four)
    far = send(far, hops=2)
    far_y = send(far_y, hops=2, yl=1)
    mine, other = sums([[[(i, s) for i in range(4)]] for s in range(2)], here, near, near_x, far_x)
    other = send(other, yl=1)

    groups = SIZES["x"] * SIZES["yh"]
    updated, kept, to_all = extract(groups, mine, other, far, far_y, momentum, u_high, u_low, v_t)
    from_all = lax.all_to_all(to_all, REP, 0, 0, tiled=True)
    new_momentum, update = finish(updated, kept, from_all, u, v_high, v_low)
    return new_momentum.reshape(1, 1, BLOCK, WIDE), update.reshape(1, BLOCK, WIDE)


def solution(mesh):
    inner = Mesh(mesh.devices.reshape(tuple(SIZES.values())), tuple(SIZES))
    in_specs = (
        P(REP, FSDP, None, None, None),
        P(REP, None, None, FSDP),
        P(None, None, FSDP, None),
    )
    out_specs = (P(REP, None, None, FSDP), P(None, None, FSDP))
    return jax.shard_map(
        per_device, mesh=inner, in_specs=in_specs, out_specs=out_specs, check_vma=False
    )
```

```python
import functools

import jax
import jax.numpy as jnp
import numpy as np
from jax import lax
from jax.experimental import pallas as pl
from jax.experimental.pallas import tpu as pltpu
from jax.sharding import Mesh
from jax.sharding import PartitionSpec as P

BLOCK = 64
BETA_DECAY = 0.999
SOFTNESS = 0.02
WIDE = 384
PAIRS = WIDE // 128
KEPT = 64
SIZES = {"x": 4, "yh": 4, "z": 8, "yl": 2, "c": 2}
REP = ("x", "yh")
FSDP = ("z", "yl", "c")
PLACES = (
    [(3, part, side) for part in range(2) for side in range(2)]
    + [(4, 0, side) for side in range(2)]
    + [(k, part, side) for k in (1, 2) for part in range(2) for side in range(2)]
    + [(0, 0, side) for side in range(2)]
)
FIRST = 10
HIGHEST = lax.Precision.HIGHEST


def dct_matrix():
    k = np.arange(BLOCK)[:, None]
    n = np.arange(BLOCK)[None, :]
    scale = np.where(k == 0, np.sqrt(1.0 / BLOCK), np.sqrt(2.0 / BLOCK))
    return (scale * np.cos(np.pi * (2 * n + 1) * k / (2 * BLOCK))).astype(np.float32)


def dot(a, b, precision=None):
    return jnp.dot(a, b, precision=precision, preferred_element_type=jnp.float32)


def halves(a):
    high = a.astype(jnp.bfloat16)
    return high, (a - high.astype(jnp.float32)).astype(jnp.bfloat16)


def dot_halves(a, b):
    return dot(a[0], b[0]) + (dot(a[1], b[0]) + dot(a[0], b[1]))


def vmem():
    return pl.BlockSpec(memory_space=pltpu.VMEM)


def f32(*shape):
    return jax.ShapeDtypeStruct(shape, jnp.float32)


def bf16(*shape):
    return jax.ShapeDtypeStruct(shape, jnp.bfloat16)


def params():
    return pltpu.CompilerParams(vmem_limit_bytes=32 * 1024 * 1024)


def pick_kernel(other, grads_ref, *outs):
    z = lax.axis_index("z")
    yl = lax.axis_index("yl")
    core = lax.axis_index("c")
    core = 1 - core if other else core
    rows = [(out, row) for out in outs for row in range(out.shape[0])]
    for (out, row), (distance, part, side) in zip(rows, PLACES):
        target = lax.rem(z + 8 + (1 - 2 * core) * distance, 8)
        block = 4 * target + 2 * (1 - yl if side else yl) + (1 - core if part else core)
        start = pl.multiple_of(block * WIDE, 128)
        out[row] = grads_ref[:, pl.ds(start, WIDE)].astype(jnp.float32)


def pick(grads, other):
    sizes = (FIRST, len(PLACES) - FIRST)
    return pl.pallas_call(
        functools.partial(pick_kernel, other),
        out_shape=tuple(f32(n, BLOCK, WIDE) for n in sizes),
        in_specs=[vmem()],
        out_specs=(vmem(),) * len(sizes),
        compiler_params=params(),
    )(grads)


def table_kernel(index_ref, dct_ref, u_ref, u_high_ref, u_low_ref, v_t_ref, v_high_ref, v_low_ref):
    dct = dct_ref[...]
    index = index_ref[...]
    size = index.shape[-1]
    iota = lax.broadcasted_iota(jnp.int32, (BLOCK, size), 0)
    hot_u = (iota == lax.shift_right_logical(index, 6)).astype(jnp.float32)
    hot_v = (iota == jnp.bitwise_and(index, 63)).astype(jnp.float32)
    twice = jnp.concatenate([dct, dct], axis=1)
    lane = lax.broadcasted_iota(jnp.int32, (size, 128), 1)
    kept = lax.broadcasted_iota(jnp.int32, (size, 128), 0)
    mine = jnp.bitwise_and(lax.shift_right_logical(kept, 5), 1) == lax.shift_right_logical(lane, 6)
    u = dot(dct.T, hot_u, HIGHEST)
    v = jnp.where(mine, dot(hot_v.T, twice, HIGHEST), 0.0)
    for p in range(PAIRS):
        span = slice(p * KEPT, (p + 1) * KEPT)
        u_ref[p] = u[:, span]
        u_high_ref[p], u_low_ref[p] = halves(u[:, span])
        v_t_ref[p] = v[span].T
        v_high_ref[p], v_low_ref[p] = halves(v[span])


def tables(index):
    square, wide = (PAIRS, BLOCK, KEPT), (PAIRS, KEPT, 128)
    return pl.pallas_call(
        table_kernel,
        out_shape=(f32(*square), bf16(*square), bf16(*square), f32(PAIRS, 128, KEPT), bf16(*wide), bf16(*wide)),
        in_specs=[vmem()] * 2,
        out_specs=(vmem(),) * 6,
        compiler_params=params(),
    )(index, dct_matrix())


def sums_kernel(plan, *refs):
    ins, outs = refs[: len(refs) - len(plan)], refs[len(refs) - len(plan) :]
    for out, rows in zip(outs, plan):
        for row, terms in enumerate(rows):
            out[row] = functools.reduce(jnp.add, [ins[i][j] for i, j in terms])


def sums(plan, *arrays, weight=0):
    return pl.pallas_call(
        functools.partial(sums_kernel, plan),
        out_shape=tuple(f32(len(rows), BLOCK, WIDE) for rows in plan),
        in_specs=[vmem()] * len(arrays),
        out_specs=(vmem(),) * len(plan),
        compiler_params=params(),
        cost_estimate=pl.CostEstimate(flops=0, bytes_accessed=int(weight * 3.69e6) or 1, transcendentals=0),
    )(*arrays)


def extract_kernel(*refs):
    *terms, momentum_ref, u_high_ref, u_low_ref, v_t_ref, updated_ref, own_ref, kept_ref = refs
    updated = functools.reduce(jnp.add, [r[0] for r in terms]) + BETA_DECAY * momentum_ref[...]
    updated_ref[...] = updated
    columns = updated.T
    row = lax.broadcasted_iota(jnp.int32, (8, KEPT), 0)
    tile = jnp.zeros((8, KEPT), jnp.float32)
    for p in range(PAIRS):
        field = halves(columns[p * 128 : (p + 1) * 128])
        product = dot_halves(field, (u_high_ref[p], u_low_ref[p])) * v_t_ref[p]
        tile = jnp.where(row == p, jnp.sum(product, axis=0, keepdims=True), tile)
    tile = jnp.concatenate([tile, jnp.zeros((8, 128 - KEPT), jnp.float32)], axis=1)
    own_ref[...] = tile
    for r in range(kept_ref.shape[0]):
        kept_ref[r] = tile


def extract(groups, *args):
    return pl.pallas_call(
        extract_kernel,
        out_shape=(f32(BLOCK, WIDE), f32(8, 128), f32(groups, 8, 128)),
        in_specs=[vmem()] * len(args),
        out_specs=(vmem(),) * 3,
        compiler_params=params(),
    )(*args)


def finish_kernel(updated_ref, own_ref, all_ref, u_ref, v_high_ref, v_low_ref, new_ref, update_ref):
    averaged = jnp.sum(all_ref[...], axis=0) * (1.0 / all_ref.shape[0])
    own = own_ref[...]
    for p in range(PAIRS):
        span = slice(p * 128, (p + 1) * 128)
        v = (v_high_ref[p], v_low_ref[p])
        inverse = lambda kept: dot_halves(halves(u_ref[p] * kept[p : p + 1, :KEPT]), v)
        direction = inverse(averaged)
        update_ref[:, span] = direction * lax.rsqrt(direction * direction + SOFTNESS * SOFTNESS)
        new_ref[:, span] = updated_ref[:, span] - inverse(own)


def finish(*args):
    return pl.pallas_call(
        finish_kernel,
        out_shape=(f32(BLOCK, WIDE),) * 2,
        in_specs=[vmem()] * len(args),
        out_specs=(vmem(),) * 2,
        compiler_params=params(),
    )(*args)


def permutation(hops, flip_yl, flip_c):
    flat = lambda z, yl, c: (z % 8) * 4 + yl * 2 + c
    return [
        (flat(z, yl, c), flat(z + hops * (1 - 2 * c), yl ^ flip_yl, c ^ flip_c))
        for z in range(8)
        for yl in range(2)
        for c in range(2)
    ]


def send(array, hops=0, yl=0, c=0):
    return lax.ppermute(array, FSDP, permutation(hops, yl, c))


def per_device(partial_grads, momentum, keep_index):
    grads = partial_grads.reshape(BLOCK, -1)
    momentum = momentum.reshape(BLOCK, WIDE)

    first, rest = pick(grads, True)
    first = send(first, c=1)
    rest = send(rest, c=1)
    own, own_rest = pick(grads, False)
    u, u_high, u_low, v_t, v_high, v_low = tables(keep_index.reshape(1, -1))
    join = lambda *slots: [[(0, i), (1, i)] for i in slots]
    three, four, near, near_x = sums([join(0, 1, 2, 3), join(4, 5), join(6, 7), join(8, 9)], own, first)
    two, here = sums([join(0, 1, 2, 3), join(4, 5)], own_rest, rest)
    three = send(three, hops=1)
    four = send(four, hops=2)
    near = send(near, hops=1)
    near_x = send(near_x, hops=1, c=1)
    (far_x,) = sums([[[(0, 2 + s), (1, 2 + s)] for s in range(2)]], two, three)
    far_x = send(far_x, hops=2, c=1)
    far, far_y = sums([[[(0, s), (1, s), (2, s)]] for s in range(2)], two, three, four)
    far = send(far, hops=2)
    far_y = send(far_y, hops=2, yl=1)
    mine, other = sums([[[(i, s) for i in range(4)]] for s in range(2)], here, near, near_x, far_x)
    other = send(other, yl=1)

    groups = SIZES["x"] * SIZES["yh"]
    updated, kept, to_all = extract(groups, mine, other, far, far_y, momentum, u_high, u_low, v_t)
    from_all = lax.all_to_all(to_all, REP, 0, 0, tiled=True)
    new_momentum, update = finish(updated, kept, from_all, u, v_high, v_low)
    return new_momentum.reshape(1, 1, BLOCK, WIDE), update.reshape(1, BLOCK, WIDE)


def solution(mesh):
    inner = Mesh(mesh.devices.reshape(tuple(SIZES.values())), tuple(SIZES))
    in_specs = (
        P(REP, FSDP, None, None, None),
        P(REP, None, None, FSDP),
        P(None, None, FSDP, None),
    )
    out_specs = (P(REP, None, None, FSDP), P(None, None, FSDP))
    return jax.shard_map(
        per_device, mesh=inner, in_specs=in_specs, out_specs=out_specs, check_vma=False
    )
```
